32 devices in a mesh: dp: 16 (over z, y, core), tensor: 2 (over x).
Axes of the slice: x: 2, y: 2, z: 4, core: 2. Of those that a mesh axis runs over, the one named last changes fastest.
Arguments:
- inputs: bfloat16 [16, 1024, 1024], P('dp', 'tensor'), may hold values from -6 to 6
- conditioning: bfloat16 [16, 1024], P('dp'), may hold values from -6 to 6
- mod_weight: bfloat16 [1024, 6, 1024], P(None, None, 'tensor'), may hold values from -0.1875 to 0.1875
- mod_bias: float32 [6, 1024], P(None, 'tensor'), may hold values from -1.8 to 1.8
- qkv_weight: bfloat16 [1024, 3, 1024], P(None, None, 'tensor'), may hold values from -0.1875 to 0.1875
- out_weight: bfloat16 [1024, 1024], P('tensor'), may hold values from -0.75 to 0.75
- up_projection_weight: bfloat16 [1024, 4096], P(None, 'tensor'), may hold values from -0.1875 to 0.1875
- down_projection_weight: bfloat16 [4096, 1024], P('tensor'), may hold values from -0.09375 to 0.09375
- cotangent: bfloat16 [16, 1024, 1024], P('dp', 'tensor'), may hold values from -6 to 6
Outputs:
- block_out: bfloat16 [16, 1024, 1024], P('dp', 'tensor')
- grad_inputs: bfloat16 [16, 1024, 1024], P('dp', 'tensor')
- grad_conditioning: float32 [16, 1024], P('dp')
- grad_mod_weight: float32 [1024, 6, 1024], P(None, None, 'tensor')
- grad_mod_bias: float32 [6, 1024], P(None, 'tensor')
- grad_qkv_weight: float32 [1024, 3, 1024], P(None, None, 'tensor')
- grad_out_weight: float32 [1024, 1024], P('tensor')
- grad_up_weight: float32 [1024, 4096], P(None, 'tensor')
- grad_down_weight: float32 [4096, 1024], P('tensor')
The draws below stay inside these ranges and needn't reach their ends.
All inputs are finite; a program needn't handle non-finite values.
Results may differ from the reference program's by a relative error of at most 0.023.
Values may be sent and summed in bfloat16 or wider, within the bound.
A program may use at most 192 MiB of HBM per device.

```python
import jax
import jax.numpy as jnp
from jax import lax

D = 1024
FF = 4096
HD = 64
SEQ = 1024
LATENTS = 16


def shard_levels(stream_key, shape, cuts, smallest, top_value):
    gain = 1.0
    for axis_at, blocks in cuts:
        heights = jax.random.uniform(jax.random.fold_in(jax.random.fold_in(stream_key, 6), axis_at), (blocks,), jnp.float32, smallest / len(cuts), top_value / len(cuts))
        gain = gain * jnp.repeat(jnp.exp(heights), shape[axis_at] // blocks).reshape((-1,) + (1,) * (len(shape) - 1 - axis_at))
    return gain


def centred(key, dims, scale, limit, cuts=(), held_as=jnp.bfloat16):
    values = jax.random.normal(key, dims, jnp.float32) * scale
    if len(cuts) > 0:
        values = shard_levels(key, dims, cuts, -0.22, 0.18) * values
    return jnp.clip(values, min=-limit, max=limit).astype(held_as)


def setup_inputs(seed: int = 0) -> dict:
    splits = jax.random.split(jax.random.key(seed), 10)
    return {
        "inputs": centred(splits[0], (LATENTS, SEQ, D), 1.0, 6.0, ((0, 16), (1, 2))),
        "conditioning": centred(splits[1], (LATENTS, D), 1.0, 6.0, ((0, 16),)),
        "mod_weight": centred(splits[2], (D, 6, D), D ** -0.5, 0.1875, ((2, 2),)),
        "mod_bias": centred(splits[3], (6, D), 0.3, 1.8, ((1, 2),), jnp.float32),
        "qkv_weight": centred(splits[4], (D, 3, D), D ** -0.5, 0.1875, ((2, 2),)),
        "out_weight": centred(splits[5], (D, D), (D // 16) ** -0.5, 0.75, ((0, 2),)),
        "up_projection_weight": centred(splits[6], (D, FF), D ** -0.5, 0.1875, ((1, 2),)),
        "down_projection_weight": centred(splits[7], (FF, D), FF ** -0.5, 0.09375, ((0, 2),)),
        "cotangent": centred(splits[8], (LATENTS, SEQ, D), 1.0, 6.0, ((0, 16), (1, 2))),
    }


@jax.custom_vjp
def low(v):
    return lax.optimization_barrier(v.astype(jnp.bfloat16)).astype(jnp.float32)

@jax.custom_vjp
def low_back(v):
    return v

def low_keep(v):
    return (low(v), None)

def low_pass(kept, grad):
    return (grad,)

def back_keep(v):
    return (v, None)

def back_low(kept, grad):
    return (low(grad),)
low.defvjp(low_keep, low_pass)
low_back.defvjp(back_keep, back_low)
highest = lax.Precision.HIGHEST
norm_eps = 1e-06

def rounded_both(values_in):
    return low_back(low(values_in))

def modulate(values_in, offset, stretch):
    center = lax.optimization_barrier(jnp.mean(values_in, axis=-1, keepdims=True))
    deviate = values_in - center
    spread = lax.optimization_barrier(jnp.mean(deviate * deviate, axis=-1, keepdims=True))
    return deviate * lax.rsqrt(spread + norm_eps) * (1.0 + stretch) + offset

def attention(query, keys, values):
    length = query.shape[0]
    block_rows = min(512, length)
    scale_factor = query.shape[2] ** (-0.5)

    def one_block(qblock):
        scores = low_back(jnp.einsum('qhd,khd->hqk', qblock, keys, precision=highest) * scale_factor)
        shares = low(jax.nn.softmax(scores, axis=-1))
        return jnp.einsum('hqk,khd->qhd', shares, values, precision=highest)
    blocks = query.reshape(length // block_rows, block_rows, query.shape[1], query.shape[2])
    results = lax.map(jax.checkpoint(one_block), blocks)
    return results.reshape(query.shape)

def block_forward(inputs, conditioning, mod_weight, mod_bias, qkv_weight, out_weight, up_projection_weight, down_projection_weight):
    length, width = inputs.shape
    head_count = width // HD
    cond_act = low(jax.nn.silu(conditioning))
    modulation = low_back(jnp.einsum('d,dkc->kc', cond_act, mod_weight, precision=highest) + mod_bias)
    normed_one = low(modulate(inputs, modulation[0], modulation[1]))
    projected = jnp.einsum('sd,dkc->skc', normed_one, qkv_weight, precision=highest)
    query = rounded_both(projected[:, 0]).reshape(length, head_count, HD)
    keys = rounded_both(projected[:, 1]).reshape(length, head_count, HD)
    values = rounded_both(projected[:, 2]).reshape(length, head_count, HD)
    attended = rounded_both(attention(query, keys, values).reshape(length, width))
    branch_attn = low_back(jnp.dot(attended, out_weight, precision=highest))
    middle = inputs + modulation[2] * branch_attn
    normed_two = low(modulate(middle, modulation[3], modulation[4]))
    hidden_pre = low_back(jnp.dot(normed_two, up_projection_weight, precision=highest))
    hidden_activation = low(jax.nn.gelu(hidden_pre, approximate=True))
    branch_mlp = low_back(jnp.dot(hidden_activation, down_projection_weight, precision=highest))
    return middle + modulation[5] * branch_mlp

def reference(inputs, conditioning, mod_weight, mod_bias, qkv_weight, out_weight, up_projection_weight, down_projection_weight, cotangent):
    weight_list = (mod_weight.astype(jnp.float32), mod_bias.astype(jnp.float32), qkv_weight.astype(jnp.float32), out_weight.astype(jnp.float32), up_projection_weight.astype(jnp.float32), down_projection_weight.astype(jnp.float32))

    def per_latent(running, pieces):
        latent, cond_row, cot_rows = pieces
        result, backward = jax.vjp(block_forward, latent.astype(jnp.float32), cond_row.astype(jnp.float32), *weight_list)
        gradients = backward(cot_rows.astype(jnp.float32))
        running = tuple((total + grad_one for total, grad_one in zip(running, gradients[2:])))
        return (running, (result.astype(jnp.bfloat16), gradients[0].astype(jnp.bfloat16), gradients[1]))
    zeroes = tuple((jnp.zeros_like(single) for single in weight_list))
    totals, outputs = lax.scan(per_latent, zeroes, (inputs, conditioning, cotangent))
    return (outputs[0], outputs[1], outputs[2], totals[0], totals[1], totals[2], totals[3], totals[4], totals[5])
```

```python
import jax
import jax.numpy as jnp
from jax import lax
from jax.experimental import pallas as pl
from jax.experimental.pallas import tpu as pltpu
from jax.sharding import PartitionSpec as P

HD = 64


norm_eps = 1e-06


def modulate(values_in, offset, stretch):
    center = jnp.mean(values_in, axis=-1, keepdims=True)
    deviate = values_in - center
    spread = jnp.mean(deviate * deviate, axis=-1, keepdims=True)
    return deviate * lax.rsqrt(spread + norm_eps) * (1.0 + stretch) + offset


def gelu_tanh(values_in):
    return jax.nn.gelu(values_in, approximate=True)


def attend_forward(query, keys, values, scale_factor, block_rows):
    length = query.shape[0]
    blocks = query.reshape(length // block_rows, block_rows, query.shape[1], query.shape[2])

    def one_block(qblock):
        scores = (
            jnp.einsum("qhd,khd->hqk", qblock, keys, preferred_element_type=jnp.float32)
            * scale_factor
        )
        row_peak = jnp.max(scores, axis=-1, keepdims=True)
        exponent = jnp.exp(scores - row_peak)
        row_total = jnp.sum(exponent, axis=-1, keepdims=True)
        shares = (exponent / row_total).astype(jnp.bfloat16)
        result = jnp.einsum("hqk,khd->qhd", shares, values, preferred_element_type=jnp.float32)
        return (result, row_peak[..., 0] + jnp.log(row_total[..., 0]))

    results, log_totals = lax.map(one_block, blocks)
    return (results.reshape(query.shape), log_totals)


def attend_backward(query, keys, values, grad_out, log_totals, scale_factor, block_rows):
    length, head_count, head_size = query.shape
    block_count = length // block_rows
    qblocks = query.reshape(block_count, block_rows, head_count, head_size)
    gblocks = grad_out.reshape(block_count, block_rows, head_count, head_size)

    def one_block(running, pieces):
        grad_keys, grad_values = running
        qblock, gblock, lblock = pieces
        scores = (
            jnp.einsum("qhd,khd->hqk", qblock, keys, preferred_element_type=jnp.float32)
            * scale_factor
        )
        shares = jnp.exp(scores - lblock[..., None])
        grad_shares = jnp.einsum("qhd,khd->hqk", gblock, values, preferred_element_type=jnp.float32)
        inner_sum = jnp.sum(shares * grad_shares, axis=-1, keepdims=True)
        grad_scores = (shares * (grad_shares - inner_sum)).astype(jnp.bfloat16)
        grad_query = (
            jnp.einsum("hqk,khd->qhd", grad_scores, keys, preferred_element_type=jnp.float32)
            * scale_factor
        )
        grad_keys = (
            grad_keys
            + jnp.einsum("hqk,qhd->khd", grad_scores, qblock, preferred_element_type=jnp.float32)
            * scale_factor
        )
        grad_values = grad_values + jnp.einsum(
            "hqk,qhd->khd", shares.astype(jnp.bfloat16), gblock, preferred_element_type=jnp.float32
        )
        return ((grad_keys, grad_values), grad_query.astype(jnp.bfloat16))

    zeroes = jnp.zeros((length, head_count, head_size), jnp.float32)
    finals, grad_query = lax.scan(one_block, (zeroes, zeroes), (qblocks, gblocks, log_totals))
    return (
        grad_query.reshape(query.shape),
        finals[0].astype(jnp.bfloat16),
        finals[1].astype(jnp.bfloat16),
    )


def body_general(
    inputs,
    conditioning,
    mod_weight,
    mod_bias,
    qkv_weight,
    out_weight,
    up_projection_weight,
    down_projection_weight,
    cotangent,
):
    latent_rows, local_len, width = inputs.shape
    local_cols = qkv_weight.shape[2]
    head_count = local_cols // HD
    length = local_len * lax.axis_size("tensor")
    block_rows = min(512, length)
    scale_factor = HD ** (-0.5)
    cond_float = conditioning.astype(jnp.float32)
    cond_silu, back_silu = jax.vjp(jax.nn.silu, cond_float)
    cond_act = cond_silu.astype(jnp.bfloat16)
    mod_local = (
        jnp.einsum("ld,dkc->lkc", cond_act, mod_weight, preferred_element_type=jnp.float32)
        + mod_bias[None]
    )
    modulation = lax.all_gather(mod_local, "tensor", axis=2, tiled=True)
    shift_one = modulation[:, 0:1, :]
    scale_one = modulation[:, 1:2, :]
    gate_one = modulation[:, 2:3, :]
    shift_two = modulation[:, 3:4, :]
    scale_two = modulation[:, 4:5, :]
    gate_two = modulation[:, 5:6, :]
    inputs_float = inputs.astype(jnp.float32)
    normed_float, back_one = jax.vjp(modulate, inputs_float, shift_one, scale_one)
    normed_one = normed_float.astype(jnp.bfloat16)
    normed_all = lax.all_gather(normed_one, "tensor", axis=1, tiled=True)
    projected = jnp.einsum(
        "lsd,dkc->lskc", normed_all, qkv_weight, preferred_element_type=jnp.float32
    ).astype(jnp.bfloat16)
    shaped = projected.reshape(latent_rows, length, 3, head_count, HD)

    def forward_latent(pieces):
        return attend_forward(pieces[:, 0], pieces[:, 1], pieces[:, 2], scale_factor, block_rows)

    attended, log_totals = lax.map(forward_latent, shaped)
    attended = attended.reshape(latent_rows, length, local_cols).astype(jnp.bfloat16)
    attn_terms = jnp.einsum("lsc,cd->lsd", attended, out_weight, preferred_element_type=jnp.float32)
    branch_attn = lax.psum_scatter(
        attn_terms.astype(jnp.bfloat16), "tensor", scatter_dimension=1, tiled=True
    ).astype(jnp.float32)
    middle = inputs_float + gate_one * branch_attn
    normed_float_two, back_two = jax.vjp(modulate, middle, shift_two, scale_two)
    normed_two = normed_float_two.astype(jnp.bfloat16)
    grad_out = cotangent.astype(jnp.float32)
    normed_second_gathered, cot_all = (
        lax.all_gather(normed_two, "tensor", axis=1, tiled=True),
        lax.all_gather(cotangent, "tensor", axis=1, tiled=True),
    )
    hidden_pre = jnp.einsum(
        "vwb,bj->vwj",
        normed_second_gathered,
        up_projection_weight,
        preferred_element_type=jnp.float32,
    )
    hidden_float, back_gelu = jax.vjp(gelu_tanh, hidden_pre)
    hidden_activation = hidden_float.astype(jnp.bfloat16)
    mlp_terms = jnp.einsum(
        "ewy,yz->ewz", hidden_activation, down_projection_weight, preferred_element_type=jnp.float32
    )
    branch_mlp = lax.psum_scatter(
        mlp_terms.astype(jnp.bfloat16), "tensor", scatter_dimension=1, tiled=True
    ).astype(jnp.float32)
    grad_feedforward = (gate_two * cot_all.astype(jnp.float32)).astype(jnp.bfloat16)
    grad_down_projection = jnp.einsum(
        "noi,nok->ik", hidden_activation, grad_feedforward, preferred_element_type=jnp.float32
    )
    grad_activation = jnp.einsum(
        "euz,hz->euh", grad_feedforward, down_projection_weight, preferred_element_type=jnp.float32
    )
    grad_preactivation = back_gelu(grad_activation)[0].astype(jnp.bfloat16)
    grad_up = jnp.einsum(
        "pae,paz->ez",
        normed_second_gathered,
        grad_preactivation,
        preferred_element_type=jnp.float32,
    )
    normed_terms = jnp.einsum(
        "qmt,zt->qmz", grad_preactivation, up_projection_weight, preferred_element_type=jnp.float32
    )
    grad_normed_two = lax.psum_scatter(
        normed_terms.astype(jnp.bfloat16), "tensor", scatter_dimension=1, tiled=True
    ).astype(jnp.float32)
    block_out = (middle + gate_two * branch_mlp).astype(jnp.bfloat16)
    grad_gate_two = jnp.sum(grad_out * branch_mlp, axis=1, keepdims=True)
    middle_back, grad_shift_two, grad_scale_two = back_two(grad_normed_two)
    grad_middle = grad_out + middle_back
    grad_gate_one = jnp.sum(grad_middle * branch_attn, axis=1, keepdims=True)
    grad_attn = (gate_one * grad_middle).astype(jnp.bfloat16)
    grad_attn_all = lax.all_gather(grad_attn, "tensor", axis=1, tiled=True)
    grad_out_weight = jnp.einsum(
        "lsc,lsd->cd", attended, grad_attn_all, preferred_element_type=jnp.float32
    )
    grad_attended = jnp.einsum(
        "lsd,cd->lsc", grad_attn_all, out_weight, preferred_element_type=jnp.float32
    ).astype(jnp.bfloat16)
    grad_shaped = grad_attended.reshape(latent_rows, length, head_count, HD)

    def backward_latent(pieces):
        qkv_rows, grad_rows, totals_rows = pieces
        return attend_backward(
            qkv_rows[:, 0],
            qkv_rows[:, 1],
            qkv_rows[:, 2],
            grad_rows,
            totals_rows,
            scale_factor,
            block_rows,
        )

    grad_query, grad_keys, grad_values = lax.map(backward_latent, (shaped, grad_shaped, log_totals))
    grad_qkv = jnp.stack((grad_query, grad_keys, grad_values), axis=2).reshape(
        latent_rows, length, 3, local_cols
    )
    grad_qkv_weight = jnp.einsum(
        "lsd,lskc->dkc", normed_all, grad_qkv, preferred_element_type=jnp.float32
    )
    normed_one_terms = jnp.einsum(
        "lskc,dkc->lsd", grad_qkv, qkv_weight, preferred_element_type=jnp.float32
    )
    grad_normed_one = lax.psum_scatter(
        normed_one_terms.astype(jnp.bfloat16), "tensor", scatter_dimension=1, tiled=True
    ).astype(jnp.float32)
    inputs_back, grad_shift_one, grad_scale_one = back_one(grad_normed_one)
    grad_inputs = (grad_middle + inputs_back).astype(jnp.bfloat16)
    modulation_terms = jnp.concatenate(
        (
            grad_shift_one,
            grad_scale_one,
            grad_gate_one,
            grad_shift_two,
            grad_scale_two,
            grad_gate_two,
        ),
        axis=1,
    )
    grad_modulation = lax.psum_scatter(
        modulation_terms.astype(jnp.bfloat16), "tensor", scatter_dimension=2, tiled=True
    )
    grad_mod_weight = jnp.einsum(
        "ld,lkc->dkc", cond_act, grad_modulation, preferred_element_type=jnp.float32
    )
    grad_mod_bias = jnp.sum(grad_modulation.astype(jnp.float32), axis=0)
    cond_terms = jnp.einsum(
        "lkc,dkc->ld", grad_modulation, mod_weight, preferred_element_type=jnp.float32
    )
    grad_cond_act = lax.psum(cond_terms, "tensor")
    grad_conditioning = back_silu(grad_cond_act)[0]
    summed = (
        lax.psum(grad_mod_weight.astype(jnp.bfloat16), "dp").astype(jnp.float32),
        lax.psum(grad_mod_bias.astype(jnp.bfloat16), "dp").astype(jnp.float32),
        lax.psum(grad_qkv_weight.astype(jnp.bfloat16), "dp").astype(jnp.float32),
        lax.psum(grad_out_weight.astype(jnp.bfloat16), "dp").astype(jnp.float32),
        lax.psum(grad_up.astype(jnp.bfloat16), "dp").astype(jnp.float32),
        lax.psum(grad_down_projection.astype(jnp.bfloat16), "dp").astype(jnp.float32),
    )
    return (
        block_out,
        grad_inputs,
        grad_conditioning,
        summed[0],
        summed[1],
        summed[2],
        summed[3],
        summed[4],
        summed[5],
    )

LOG2E = 1.4426950408889634
ATT_ROWS = 512


def attn_fwd_kernel(qkv_ref, out_ref, lse_ref):
    length = qkv_ref.shape[1]
    fold = LOG2E * HD ** (-0.5)
    for head in range(2):
        cols = pl.ds(head * HD, HD)
        keys = qkv_ref[1, :, cols]
        values = qkv_ref[2, :, cols]
        for start in range(0, length, ATT_ROWS):
            rows = pl.ds(start, ATT_ROWS)
            query = qkv_ref[0, rows, cols]
            scores = lax.dot_general(
                query, keys, (((1,), (1,)), ((), ())), preferred_element_type=jnp.float32
            )
            peak = jnp.max(scores, axis=-1, keepdims=True)
            exponent = jnp.exp2((scores - peak) * fold)
            total = jnp.sum(exponent, axis=-1, keepdims=True)
            shares = (exponent * (1.0 / total)).astype(jnp.bfloat16)
            result = jnp.dot(shares, values, preferred_element_type=jnp.float32)
            out_ref[rows, cols] = result.astype(jnp.bfloat16)
            log_total = peak * fold + jnp.log2(total)
            flat = jnp.transpose(jnp.broadcast_to(log_total, (ATT_ROWS, 128)))
            lse_ref[0, head : head + 1, rows] = flat[0:1]


def attn_bwd_kernel(qkv_ref, grad_ref, lse_ref, out_ref):
    length = qkv_ref.shape[1]
    scale = HD ** (-0.5)
    fold = LOG2E * scale
    for head in range(2):
        cols = pl.ds(head * HD, HD)
        query = qkv_ref[0, :, cols]
        grad = grad_ref[:, cols]
        lse = lse_ref[0, head : head + 1, :]
        keys = qkv_ref[1, :, cols]
        values = qkv_ref[2, :, cols]
        dk = jnp.zeros((length, HD), jnp.float32)
        dv = jnp.zeros((length, HD), jnp.float32)
        for start in range(0, length, ATT_ROWS):
            qblock = query[start : start + ATT_ROWS]
            gblock = grad[start : start + ATT_ROWS]
            scores = lax.dot_general(
                keys, qblock, (((1,), (1,)), ((), ())), preferred_element_type=jnp.float32
            )
            probs = jnp.exp2(scores * fold - lse[:, start : start + ATT_ROWS])
            dprobs = lax.dot_general(
                values, gblock, (((1,), (1,)), ((), ())), preferred_element_type=jnp.float32
            )
            inner = jnp.sum(probs * dprobs, axis=0, keepdims=True)
            dscores = (probs * (dprobs - inner)).astype(jnp.bfloat16)
            dv = dv + jnp.dot(probs.astype(jnp.bfloat16), gblock, preferred_element_type=jnp.float32)
            dk = dk + jnp.dot(dscores, qblock, preferred_element_type=jnp.float32)
            dq = lax.dot_general(
                dscores, keys, (((0,), (0,)), ((), ())), preferred_element_type=jnp.float32
            )
            out_ref[0, pl.ds(start, ATT_ROWS), cols] = (dq * scale).astype(jnp.bfloat16)
        out_ref[1, :, cols] = (dk * scale).astype(jnp.bfloat16)
        out_ref[2, :, cols] = dv.astype(jnp.bfloat16)


def attn_forward(qkv, first, pairs):
    _, length, _ = qkv.shape
    return pl.pallas_call(
        attn_fwd_kernel,
        grid=(pairs,),
        in_specs=[pl.BlockSpec((3, length, 2 * HD), lambda i: (0, 0, first + i))],
        out_specs=[
            pl.BlockSpec((length, 2 * HD), lambda i: (0, i)),
            pl.BlockSpec((1, 8, length), lambda i: (i, 0, 0)),
        ],
        out_shape=[
            jax.ShapeDtypeStruct((length, pairs * 2 * HD), jnp.bfloat16),
            jax.ShapeDtypeStruct((pairs, 8, length), jnp.float32),
        ],
        compiler_params=pltpu.CompilerParams(vmem_limit_bytes=48 * 1024 * 1024),
        cost_estimate=pl.CostEstimate(
            flops=pairs * 2 * 4 * length * length * HD * 4,
            bytes_accessed=pairs * 8 * length * 2 * HD,
            transcendentals=pairs * 2 * length * length,
        ),
        name="attn_fwd",
    )(qkv)


def attn_backward(qkv, grad, lse):
    _, length, local = qkv.shape
    pairs = local // (2 * HD)
    return pl.pallas_call(
        attn_bwd_kernel,
        grid=(pairs,),
        in_specs=[
            pl.BlockSpec((3, length, 2 * HD), lambda i: (0, 0, i)),
            pl.BlockSpec((length, 2 * HD), lambda i: (0, i)),
            pl.BlockSpec((1, 8, length), lambda i: (i, 0, 0)),
        ],
        out_specs=pl.BlockSpec((3, length, 2 * HD), lambda i: (0, 0, i)),
        out_shape=jax.ShapeDtypeStruct((3, length, local), jnp.bfloat16),
        compiler_params=pltpu.CompilerParams(vmem_limit_bytes=48 * 1024 * 1024),
        cost_estimate=pl.CostEstimate(
            flops=pairs * 2 * 10 * length * length * HD * 4,
            bytes_accessed=pairs * 14 * length * 2 * HD,
            transcendentals=pairs * 2 * length * length,
        ),
        name="attn_bwd",
    )(qkv, grad, lse)


def swap(values_in):
    return lax.ppermute(values_in, "tensor", ((0, 1), (1, 0)))


def dot_f32(left, right, dims):
    return lax.dot_general(left, right, (dims, ((), ())), preferred_element_type=jnp.float32)


NN = ((1,), (0,))
NT = ((1,), (1,))
TN = ((0,), (0,))


def body_pair(
    inputs,
    conditioning,
    mod_weight,
    mod_bias,
    qkv_weight,
    out_weight,
    up_projection_weight,
    down_projection_weight,
    cotangent,
):
    bf16 = jnp.bfloat16
    mine = lax.axis_index("tensor")
    x_own = inputs[0]
    half, width = x_own.shape
    local_cols = qkv_weight.shape[2]
    pairs = local_cols // (2 * HD)
    x_peer = swap(x_own)
    cond_silu, back_silu = jax.vjp(jax.nn.silu, conditioning.astype(jnp.float32))
    cond_act = cond_silu.astype(bf16)
    mod_own = (
        jnp.einsum("ld,dkc->lkc", cond_act, mod_weight, preferred_element_type=jnp.float32)
        + mod_bias[None]
    )[0]
    mod_peer = swap(mod_own)
    modulation = jnp.where(
        mine == 0,
        jnp.concatenate((mod_own, mod_peer), axis=1),
        jnp.concatenate((mod_peer, mod_own), axis=1),
    )
    shift_one, scale_one, gate_one, shift_two, scale_two, gate_two = (
        modulation[k : k + 1] for k in range(6)
    )
    xf_own = x_own.astype(jnp.float32)
    normed_own_f, back_one = jax.vjp(modulate, xf_own, shift_one, scale_one)
    normed_own = normed_own_f.astype(bf16)
    cot_later, out_later, x_peer = lax.optimization_barrier((cotangent[0], out_weight, x_peer))
    cot_peer = swap(cot_later)
    out_peer = swap(out_later)
    xf_peer = x_peer.astype(jnp.float32)
    normed_peer = modulate(xf_peer, shift_one, scale_one).astype(bf16)
    normed_one = jnp.concatenate((normed_own, normed_peer), axis=0)
    qkv = jnp.einsum(
        "sd,dkc->ksc", normed_one, qkv_weight, preferred_element_type=jnp.float32
    ).astype(bf16)
    att_a, lse_a = attn_forward(qkv, 0, pairs // 2)
    far_a = swap(att_a)
    att_b, lse_b = attn_forward(qkv, pairs // 2, pairs - pairs // 2)
    far_b = swap(att_b)
    lse = jnp.concatenate((lse_a, lse_b), axis=0)
    attended = jnp.concatenate((att_a, att_b), axis=1)
    far = jnp.concatenate((far_a, far_b), axis=1)
    both = jnp.concatenate(
        (attended, jnp.concatenate((far[half:], far[:half]), axis=0)), axis=1
    )
    branch_attn = dot_f32(both, jnp.concatenate((out_weight, out_peer), axis=0), NN)
    branch_own = branch_attn[:half]
    middle_own = xf_own + gate_one * branch_own
    middle_peer = xf_peer + gate_one * branch_attn[half:]
    normed_two_f, back_two = jax.vjp(modulate, middle_own, shift_two, scale_two)
    normed_two = jnp.concatenate(
        (normed_two_f.astype(bf16), modulate(middle_peer, shift_two, scale_two).astype(bf16)),
        axis=0,
    )
    grad_out = cotangent[0].astype(jnp.float32)
    grad_mlp = jnp.concatenate(
        (
            (gate_two * grad_out).astype(bf16),
            (gate_two * cot_peer.astype(jnp.float32)).astype(bf16),
        ),
        axis=0,
    )
    hidden_pre = dot_f32(normed_two, up_projection_weight, NN)
    hidden_f, back_gelu = jax.vjp(gelu_tanh, hidden_pre)
    hidden_act = hidden_f.astype(bf16)
    grad_act = dot_f32(grad_mlp, down_projection_weight, NT)
    grad_pre = back_gelu(grad_act)[0].astype(bf16)
    two_recv = swap(dot_f32(grad_pre[half:], up_projection_weight, NT).astype(bf16))
    two_own = dot_f32(grad_pre[:half], up_projection_weight, NT)
    grad_down = dot_f32(hidden_act, grad_mlp, TN).astype(bf16)
    grad_up = dot_f32(normed_two, grad_pre, TN).astype(bf16)
    grad_down, grad_up, two_recv = lax.optimization_barrier((grad_down, grad_up, two_recv))
    sum_down, sum_up = lax.psum((grad_down, grad_up), "dp")
    grad_normed_two = two_own + two_recv.astype(jnp.float32)
    middle_back, grad_shift_two, grad_scale_two = back_two(grad_normed_two)
    grad_middle = grad_out + middle_back
    grad_gate_one = jnp.sum(grad_middle * branch_own, axis=0, keepdims=True)
    ga_own = (gate_one * grad_middle).astype(bf16)
    ga_peer = swap(ga_own)
    mlp_far = dot_f32(hidden_act[half:], down_projection_weight, NN).astype(bf16)
    mlp_own = dot_f32(hidden_act[:half], down_projection_weight, NN)
    mlp_far, ga_peer = lax.optimization_barrier((mlp_far, ga_peer))
    branch_mlp = mlp_own + swap(mlp_far).astype(jnp.float32)
    grad_attn = jnp.concatenate((ga_own, ga_peer), axis=0)
    grad_attended = dot_f32(grad_attn, out_weight, NT).astype(bf16)
    grad_out_weight = dot_f32(attended, grad_attn, TN).astype(bf16)
    grad_qkv = attn_backward(qkv, grad_attended, lse)
    one_recv = swap(
        jnp.einsum(
            "ksc,dkc->sd", grad_qkv[:, half:], qkv_weight, preferred_element_type=jnp.float32
        ).astype(bf16)
    )
    one_own = jnp.einsum(
        "ksc,dkc->sd", grad_qkv[:, :half], qkv_weight, preferred_element_type=jnp.float32
    )
    grad_qkv_weight = jnp.einsum(
        "sd,ksc->dkc", normed_one, grad_qkv, preferred_element_type=jnp.float32
    ).astype(bf16)
    grad_qkv_weight, grad_out_weight, sum_down, sum_up = lax.optimization_barrier(
        (grad_qkv_weight, grad_out_weight, sum_down, sum_up)
    )
    sum_qkv, sum_out = lax.psum((grad_qkv_weight, grad_out_weight), "dp")
    block_out = (middle_own + gate_two * branch_mlp).astype(bf16)
    grad_gate_two = jnp.sum(grad_out * branch_mlp, axis=0, keepdims=True)
    grad_normed_one = one_own + one_recv.astype(jnp.float32)
    inputs_back, grad_shift_one, grad_scale_one = back_one(grad_normed_one)
    grad_inputs = (grad_middle + inputs_back).astype(bf16)
    mod_terms = jnp.concatenate(
        (
            grad_shift_one,
            grad_scale_one,
            grad_gate_one,
            grad_shift_two,
            grad_scale_two,
            grad_gate_two,
        ),
        axis=0,
    )
    left, right = mod_terms[:, :local_cols], mod_terms[:, local_cols:]
    mod_keep = jnp.where(mine == 0, left, right)
    mod_send = jnp.where(mine == 0, right, left).astype(bf16)
    grad_mod = (mod_keep + swap(mod_send).astype(jnp.float32)).astype(bf16)[None]
    cond_all = lax.all_gather(cond_act, "dp", axis=0, tiled=True)
    mod_all = lax.all_gather(grad_mod, "dp", axis=0, tiled=True)
    grad_mod_weight = jnp.einsum(
        "ld,lkc->dkc", cond_all, mod_all, preferred_element_type=jnp.float32
    )
    grad_mod_bias = jnp.sum(mod_all.astype(jnp.float32), axis=0)
    cond_terms = jnp.einsum(
        "lkc,dkc->ld", grad_mod, mod_weight, preferred_element_type=jnp.float32
    )
    grad_conditioning = back_silu(cond_terms + swap(cond_terms))[0]
    return (
        block_out[None],
        grad_inputs[None],
        grad_conditioning,
        grad_mod_weight,
        grad_mod_bias,
        sum_qkv.astype(jnp.float32),
        sum_out.astype(jnp.float32),
        sum_up.astype(jnp.float32),
        sum_down.astype(jnp.float32),
    )


def body(inputs, conditioning, mod_weight, mod_bias, qkv_weight, *rest):
    fits = inputs.shape[1] % 256 == 0 and qkv_weight.shape[2] % (4 * HD) == 0
    if lax.axis_size("tensor") == 2 and inputs.shape[0] == 1 and fits:
        return body_pair(inputs, conditioning, mod_weight, mod_bias, qkv_weight, *rest)
    return body_general(inputs, conditioning, mod_weight, mod_bias, qkv_weight, *rest)


def solution(mesh):
    return jax.shard_map(
        body,
        mesh=mesh,
        in_specs=(
            P("dp", "tensor", None),
            P("dp", None),
            P(None, None, "tensor"),
            P(None, "tensor"),
            P(None, None, "tensor"),
            P("tensor", None),
            P(None, "tensor"),
            P("tensor", None),
            P("dp", "tensor", None),
        ),
        out_specs=(
            P("dp", "tensor", None),
            P("dp", "tensor", None),
            P("dp", None),
            P(None, None, "tensor"),
            P(None, "tensor"),
            P(None, None, "tensor"),
            P("tensor", None),
            P(None, "tensor"),
            P("tensor", None),
        ),
        check_vma=False,
    )
```

```python
import jax
import jax.numpy as jnp
from jax import lax
from jax.experimental import pallas as pl
from jax.experimental.pallas import tpu as pltpu
from jax.sharding import PartitionSpec as P

HD = 64


norm_eps = 1e-06


def modulate(values_in, offset, stretch):
    center = jnp.mean(values_in, axis=-1, keepdims=True)
    deviate = values_in - center
    spread = jnp.mean(deviate * deviate, axis=-1, keepdims=True)
    return deviate * lax.rsqrt(spread + norm_eps) * (1.0 + stretch) + offset


def gelu_tanh(values_in):
    return jax.nn.gelu(values_in, approximate=True)


def attend_forward(query, keys, values, scale_factor, block_rows):
    length = query.shape[0]
    blocks = query.reshape(length // block_rows, block_rows, query.shape[1], query.shape[2])

    def one_block(qblock):
        scores = (
            jnp.einsum("qhd,khd->hqk", qblock, keys, preferred_element_type=jnp.float32)
            * scale_factor
        )
        row_peak = jnp.max(scores, axis=-1, keepdims=True)
        exponent = jnp.exp(scores - row_peak)
        row_total = jnp.sum(exponent, axis=-1, keepdims=True)
        shares = (exponent / row_total).astype(jnp.bfloat16)
        result = jnp.einsum("hqk,khd->qhd", shares, values, preferred_element_type=jnp.float32)
        return (result, row_peak[..., 0] + jnp.log(row_total[..., 0]))

    results, log_totals = lax.map(one_block, blocks)
    return (results.reshape(query.shape), log_totals)


def attend_backward(query, keys, values, grad_out, log_totals, scale_factor, block_rows):
    length, head_count, head_size = query.shape
    block_count = length // block_rows
    qblocks = query.reshape(block_count, block_rows, head_count, head_size)
    gblocks = grad_out.reshape(block_count, block_rows, head_count, head_size)

    def one_block(running, pieces):
        grad_keys, grad_values = running
        qblock, gblock, lblock = pieces
        scores = (
            jnp.einsum("qhd,khd->hqk", qblock, keys, preferred_element_type=jnp.float32)
            * scale_factor
        )
        shares = jnp.exp(scores - lblock[..., None])
        grad_shares = jnp.einsum("qhd,khd->hqk", gblock, values, preferred_element_type=jnp.float32)
        inner_sum = jnp.sum(shares * grad_shares, axis=-1, keepdims=True)
        grad_scores = (shares * (grad_shares - inner_sum)).astype(jnp.bfloat16)
        grad_query = (
            jnp.einsum("hqk,khd->qhd", grad_scores, keys, preferred_element_type=jnp.float32)
            * scale_factor
        )
        grad_keys = (
            grad_keys
            + jnp.einsum("hqk,qhd->khd", grad_scores, qblock, preferred_element_type=jnp.float32)
            * scale_factor
        )
        grad_values = grad_values + jnp.einsum(
            "hqk,qhd->khd", shares.astype(jnp.bfloat16), gblock, preferred_element_type=jnp.float32
        )
        return ((grad_keys, grad_values), grad_query.astype(jnp.bfloat16))

    zeroes = jnp.zeros((length, head_count, head_size), jnp.float32)
    finals, grad_query = lax.scan(one_block, (zeroes, zeroes), (qblocks, gblocks, log_totals))
    return (
        grad_query.reshape(query.shape),
        finals[0].astype(jnp.bfloat16),
        finals[1].astype(jnp.bfloat16),
    )


def body_general(
    inputs,
    conditioning,
    mod_weight,
    mod_bias,
    qkv_weight,
    out_weight,
    up_projection_weight,
    down_projection_weight,
    cotangent,
):
    latent_rows, local_len, width = inputs.shape
    local_cols = qkv_weight.shape[2]
    head_count = local_cols // HD
    length = local_len * lax.axis_size("tensor")
    block_rows = min(512, length)
    scale_factor = HD ** (-0.5)
    cond_float = conditioning.astype(jnp.float32)
    cond_silu, back_silu = jax.vjp(jax.nn.silu, cond_float)
    cond_act = cond_silu.astype(jnp.bfloat16)
    mod_local = (
        jnp.einsum("ld,dkc->lkc", cond_act, mod_weight, preferred_element_type=jnp.float32)
        + mod_bias[None]
    )
    modulation = lax.all_gather(mod_local, "tensor", axis=2, tiled=True)
    shift_one = modulation[:, 0:1, :]
    scale_one = modulation[:, 1:2, :]
    gate_one = modulation[:, 2:3, :]
    shift_two = modulation[:, 3:4, :]
    scale_two = modulation[:, 4:5, :]
    gate_two = modulation[:, 5:6, :]
    inputs_float = inputs.astype(jnp.float32)
    normed_float, back_one = jax.vjp(modulate, inputs_float, shift_one, scale_one)
    normed_one = normed_float.astype(jnp.bfloat16)
    normed_all = lax.all_gather(normed_one, "tensor", axis=1, tiled=True)
    projected = jnp.einsum(
        "lsd,dkc->lskc", normed_all, qkv_weight, preferred_element_type=jnp.float32
    ).astype(jnp.bfloat16)
    shaped = projected.reshape(latent_rows, length, 3, head_count, HD)

    def forward_latent(pieces):
        return attend_forward(pieces[:, 0], pieces[:, 1], pieces[:, 2], scale_factor, block_rows)

    attended, log_totals = lax.map(forward_latent, shaped)
    attended = attended.reshape(latent_rows, length, local_cols).astype(jnp.bfloat16)
    attn_terms = jnp.einsum("lsc,cd->lsd", attended, out_weight, preferred_element_type=jnp.float32)
    branch_attn = lax.psum_scatter(
        attn_terms.astype(jnp.bfloat16), "tensor", scatter_dimension=1, tiled=True
    ).astype(jnp.float32)
    middle = inputs_float + gate_one * branch_attn
    normed_float_two, back_two = jax.vjp(modulate, middle, shift_two, scale_two)
    normed_two = normed_float_two.astype(jnp.bfloat16)
    grad_out = cotangent.astype(jnp.float32)
    normed_second_gathered, cot_all = (
        lax.all_gather(normed_two, "tensor", axis=1, tiled=True),
        lax.all_gather(cotangent, "tensor", axis=1, tiled=True),
    )
    hidden_pre = jnp.einsum(
        "vwb,bj->vwj",
        normed_second_gathered,
        up_projection_weight,
        preferred_element_type=jnp.float32,
    )
    hidden_float, back_gelu = jax.vjp(gelu_tanh, hidden_pre)
    hidden_activation = hidden_float.astype(jnp.bfloat16)
    mlp_terms = jnp.einsum(
        "ewy,yz->ewz", hidden_activation, down_projection_weight, preferred_element_type=jnp.float32
    )
    branch_mlp = lax.psum_scatter(
        mlp_terms.astype(jnp.bfloat16), "tensor", scatter_dimension=1, tiled=True
    ).astype(jnp.float32)
    grad_feedforward = (gate_two * cot_all.astype(jnp.float32)).astype(jnp.bfloat16)
    grad_down_projection = jnp.einsum(
        "noi,nok->ik", hidden_activation, grad_feedforward, preferred_element_type=jnp.float32
    )
    grad_activation = jnp.einsum(
        "euz,hz->euh", grad_feedforward, down_projection_weight, preferred_element_type=jnp.float32
    )
    grad_preactivation = back_gelu(grad_activation)[0].astype(jnp.bfloat16)
    grad_up = jnp.einsum(
        "pae,paz->ez",
        normed_second_gathered,
        grad_preactivation,
        preferred_element_type=jnp.float32,
    )
    normed_terms = jnp.einsum(
        "qmt,zt->qmz", grad_preactivation, up_projection_weight, preferred_element_type=jnp.float32
    )
    grad_normed_two = lax.psum_scatter(
        normed_terms.astype(jnp.bfloat16), "tensor", scatter_dimension=1, tiled=True
    ).astype(jnp.float32)
    block_out = (middle + gate_two * branch_mlp).astype(jnp.bfloat16)
    grad_gate_two = jnp.sum(grad_out * branch_mlp, axis=1, keepdims=True)
    middle_back, grad_shift_two, grad_scale_two = back_two(grad_normed_two)
    grad_middle = grad_out + middle_back
    grad_gate_one = jnp.sum(grad_middle * branch_attn, axis=1, keepdims=True)
    grad_attn = (gate_one * grad_middle).astype(jnp.bfloat16)
    grad_attn_all = lax.all_gather(grad_attn, "tensor", axis=1, tiled=True)
    grad_out_weight = jnp.einsum(
        "lsc,lsd->cd", attended, grad_attn_all, preferred_element_type=jnp.float32
    )
    grad_attended = jnp.einsum(
        "lsd,cd->lsc", grad_attn_all, out_weight, preferred_element_type=jnp.float32
    ).astype(jnp.bfloat16)
    grad_shaped = grad_attended.reshape(latent_rows, length, head_count, HD)

    def backward_latent(pieces):
        qkv_rows, grad_rows, totals_rows = pieces
        return attend_backward(
            qkv_rows[:, 0],
            qkv_rows[:, 1],
            qkv_rows[:, 2],
            grad_rows,
            totals_rows,
            scale_factor,
            block_rows,
        )

    grad_query, grad_keys, grad_values = lax.map(backward_latent, (shaped, grad_shaped, log_totals))
    grad_qkv = jnp.stack((grad_query, grad_keys, grad_values), axis=2).reshape(
        latent_rows, length, 3, local_cols
    )
    grad_qkv_weight = jnp.einsum(
        "lsd,lskc->dkc", normed_all, grad_qkv, preferred_element_type=jnp.float32
    )
    normed_one_terms = jnp.einsum(
        "lskc,dkc->lsd", grad_qkv, qkv_weight, preferred_element_type=jnp.float32
    )
    grad_normed_one = lax.psum_scatter(
        normed_one_terms.astype(jnp.bfloat16), "tensor", scatter_dimension=1, tiled=True
    ).astype(jnp.float32)
    inputs_back, grad_shift_one, grad_scale_one = back_one(grad_normed_one)
    grad_inputs = (grad_middle + inputs_back).astype(jnp.bfloat16)
    modulation_terms = jnp.concatenate(
        (
            grad_shift_one,
            grad_scale_one,
            grad_gate_one,
            grad_shift_two,
            grad_scale_two,
            grad_gate_two,
        ),
        axis=1,
    )
    grad_modulation = lax.psum_scatter(
        modulation_terms.astype(jnp.bfloat16), "tensor", scatter_dimension=2, tiled=True
    )
    grad_mod_weight = jnp.einsum(
        "ld,lkc->dkc", cond_act, grad_modulation, preferred_element_type=jnp.float32
    )
    grad_mod_bias = jnp.sum(grad_modulation.astype(jnp.float32), axis=0)
    cond_terms = jnp.einsum(
        "lkc,dkc->ld", grad_modulation, mod_weight, preferred_element_type=jnp.float32
    )
    grad_cond_act = lax.psum(cond_terms, "tensor")
    grad_conditioning = back_silu(grad_cond_act)[0]
    summed = (
        lax.psum(grad_mod_weight.astype(jnp.bfloat16), "dp").astype(jnp.float32),
        lax.psum(grad_mod_bias.astype(jnp.bfloat16), "dp").astype(jnp.float32),
        lax.psum(grad_qkv_weight.astype(jnp.bfloat16), "dp").astype(jnp.float32),
        lax.psum(grad_out_weight.astype(jnp.bfloat16), "dp").astype(jnp.float32),
        lax.psum(grad_up.astype(jnp.bfloat16), "dp").astype(jnp.float32),
        lax.psum(grad_down_projection.astype(jnp.bfloat16), "dp").astype(jnp.float32),
    )
    return (
        block_out,
        grad_inputs,
        grad_conditioning,
        summed[0],
        summed[1],
        summed[2],
        summed[3],
        summed[4],
        summed[5],
    )

LOG2E = 1.4426950408889634
ATT_ROWS = 512


def attn_fwd_kernel(qkv_ref, out_ref, lse_ref):
    length = qkv_ref.shape[1]
    fold = LOG2E * HD ** (-0.5)
    for head in range(2):
        cols = pl.ds(head * HD, HD)
        keys = qkv_ref[1, :, cols]
        values = qkv_ref[2, :, cols]
        for start in range(0, length, ATT_ROWS):
            rows = pl.ds(start, ATT_ROWS)
            query = qkv_ref[0, rows, cols]
            scores = lax.dot_general(
                query, keys, (((1,), (1,)), ((), ())), preferred_element_type=jnp.float32
            )
            peak = jnp.max(scores, axis=-1, keepdims=True)
            exponent = jnp.exp2((scores - peak) * fold)
            total = jnp.sum(exponent, axis=-1, keepdims=True)
            shares = (exponent * (1.0 / total)).astype(jnp.bfloat16)
            result = jnp.dot(shares, values, preferred_element_type=jnp.float32)
            out_ref[rows, cols] = result.astype(jnp.bfloat16)
            log_total = peak * fold + jnp.log2(total)
            flat = jnp.transpose(jnp.broadcast_to(log_total, (ATT_ROWS, 128)))
            lse_ref[0, head : head + 1, rows] = flat[0:1]


def attn_bwd_kernel(qkv_ref, grad_ref, lse_ref, out_ref):
    length = qkv_ref.shape[1]
    scale = HD ** (-0.5)
    fold = LOG2E * scale
    for head in range(2):
        cols = pl.ds(head * HD, HD)
        query = qkv_ref[0, :, cols]
        grad = grad_ref[:, cols]
        lse = lse_ref[0, head : head + 1, :]
        keys = qkv_ref[1, :, cols]
        values = qkv_ref[2, :, cols]
        dk = jnp.zeros((length, HD), jnp.float32)
        dv = jnp.zeros((length, HD), jnp.float32)
        for start in range(0, length, ATT_ROWS):
            qblock = query[start : start + ATT_ROWS]
            gblock = grad[start : start + ATT_ROWS]
            scores = lax.dot_general(
                keys, qblock, (((1,), (1,)), ((), ())), preferred_element_type=jnp.float32
            )
            probs = jnp.exp2(scores * fold - lse[:, start : start + ATT_ROWS])
            dprobs = lax.dot_general(
                values, gblock, (((1,), (1,)), ((), ())), preferred_element_type=jnp.float32
            )
            inner = jnp.sum(probs * dprobs, axis=0, keepdims=True)
            dscores = (probs * (dprobs - inner)).astype(jnp.bfloat16)
            dv = dv + jnp.dot(probs.astype(jnp.bfloat16), gblock, preferred_element_type=jnp.float32)
            dk = dk + jnp.dot(dscores, qblock, preferred_element_type=jnp.float32)
            dq = lax.dot_general(
                dscores, keys, (((0,), (0,)), ((), ())), preferred_element_type=jnp.float32
            )
            out_ref[0, pl.ds(start, ATT_ROWS), cols] = (dq * scale).astype(jnp.bfloat16)
        out_ref[1, :, cols] = (dk * scale).astype(jnp.bfloat16)
        out_ref[2, :, cols] = dv.astype(jnp.bfloat16)


def attn_forward(qkv, first, pairs):
    _, length, _ = qkv.shape
    return pl.pallas_call(
        attn_fwd_kernel,
        grid=(pairs,),
        in_specs=[pl.BlockSpec((3, length, 2 * HD), lambda i: (0, 0, first + i))],
        out_specs=[
            pl.BlockSpec((length, 2 * HD), lambda i: (0, i)),
            pl.BlockSpec((1, 8, length), lambda i: (i, 0, 0)),
        ],
        out_shape=[
            jax.ShapeDtypeStruct((length, pairs * 2 * HD), jnp.bfloat16),
            jax.ShapeDtypeStruct((pairs, 8, length), jnp.float32),
        ],
        compiler_params=pltpu.CompilerParams(vmem_limit_bytes=48 * 1024 * 1024),
        cost_estimate=pl.CostEstimate(
            flops=pairs * 2 * 4 * length * length * HD * 4,
            bytes_accessed=pairs * 8 * length * 2 * HD,
            transcendentals=pairs * 2 * length * length,
        ),
        name="attn_fwd",
    )(qkv)


def attn_backward(qkv, grad, lse):
    _, length, local = qkv.shape
    pairs = local // (2 * HD)
    return pl.pallas_call(
        attn_bwd_kernel,
        grid=(pairs,),
        in_specs=[
            pl.BlockSpec((3, length, 2 * HD), lambda i: (0, 0, i)),
            pl.BlockSpec((length, 2 * HD), lambda i: (0, i)),
            pl.BlockSpec((1, 8, length), lambda i: (i, 0, 0)),
        ],
        out_specs=pl.BlockSpec((3, length, 2 * HD), lambda i: (0, 0, i)),
        out_shape=jax.ShapeDtypeStruct((3, length, local), jnp.bfloat16),
        compiler_params=pltpu.CompilerParams(vmem_limit_bytes=48 * 1024 * 1024),
        cost_estimate=pl.CostEstimate(
            flops=pairs * 2 * 10 * length * length * HD * 4,
            bytes_accessed=pairs * 14 * length * 2 * HD,
            transcendentals=pairs * 2 * length * length,
        ),
        name="attn_bwd",
    )(qkv, grad, lse)


def swap(values_in):
    return lax.ppermute(values_in, "tensor", ((0, 1), (1, 0)))


def sum_latents(values_in, order):
    count = lax.axis_size("dp")
    me = lax.axis_index("dp")
    if count != 16 or values_in.shape[0] % 256 != 0:
        return lax.psum(values_in, "dp").astype(jnp.float32)
    part = values_in
    for bit in order:
        partners = [(i, i ^ bit) for i in range(count)]
        half = part.shape[0] // 2
        mine_at = jnp.where((me & bit) != 0, half, 0)
        sent = lax.dynamic_slice_in_dim(part, half - mine_at, half, 0)
        kept = lax.dynamic_slice_in_dim(part, mine_at, half, 0)
        came = lax.ppermute(sent, "dp", partners)
        part = (kept.astype(jnp.float32) + came.astype(jnp.float32)).astype(jnp.bfloat16)
    for bit in reversed(order):
        partners = [(i, i ^ bit) for i in range(count)]
        came = lax.ppermute(part, "dp", partners)
        part = jnp.where(
            (me & bit) != 0,
            jnp.concatenate((came, part), axis=0),
            jnp.concatenate((part, came), axis=0),
        )
    return part.astype(jnp.float32)


Y_FIRST = (1, 2, 4, 8)
Z_FIRST = (1, 4, 8, 2)


def dot_f32(left, right, dims):
    return lax.dot_general(left, right, (dims, ((), ())), preferred_element_type=jnp.float32)


NN = ((1,), (0,))
NT = ((1,), (1,))
TN = ((0,), (0,))


def body_pair(
    inputs,
    conditioning,
    mod_weight,
    mod_bias,
    qkv_weight,
    out_weight,
    up_projection_weight,
    down_projection_weight,
    cotangent,
):
    bf16 = jnp.bfloat16
    mine = lax.axis_index("tensor")
    x_own = inputs[0]
    half, width = x_own.shape
    local_cols = qkv_weight.shape[2]
    pairs = local_cols // (2 * HD)
    x_peer = swap(x_own)
    cond_silu, back_silu = jax.vjp(jax.nn.silu, conditioning.astype(jnp.float32))
    cond_act = cond_silu.astype(bf16)
    mod_own = (
        jnp.einsum("ld,dkc->lkc", cond_act, mod_weight, preferred_element_type=jnp.float32)
        + mod_bias[None]
    )[0]
    mod_peer = swap(mod_own)
    modulation = jnp.where(
        mine == 0,
        jnp.concatenate((mod_own, mod_peer), axis=1),
        jnp.concatenate((mod_peer, mod_own), axis=1),
    )
    shift_one, scale_one, gate_one, shift_two, scale_two, gate_two = (
        modulation[k : k + 1] for k in range(6)
    )
    xf_own = x_own.astype(jnp.float32)
    normed_own_f, back_one = jax.vjp(modulate, xf_own, shift_one, scale_one)
    normed_own = normed_own_f.astype(bf16)
    cot_later, out_later, x_peer = lax.optimization_barrier((cotangent[0], out_weight, x_peer))
    cot_peer = swap(cot_later)
    out_peer = swap(out_later)
    xf_peer = x_peer.astype(jnp.float32)
    normed_peer = modulate(xf_peer, shift_one, scale_one).astype(bf16)
    normed_one = jnp.concatenate((normed_own, normed_peer), axis=0)
    qkv = jnp.einsum(
        "sd,dkc->ksc", normed_one, qkv_weight, preferred_element_type=jnp.float32
    ).astype(bf16)
    att_a, lse_a = attn_forward(qkv, 0, pairs // 2)
    far_a = swap(att_a)
    att_b, lse_b = attn_forward(qkv, pairs // 2, pairs - pairs // 2)
    far_b = swap(att_b)
    lse = jnp.concatenate((lse_a, lse_b), axis=0)
    attended = jnp.concatenate((att_a, att_b), axis=1)
    far = jnp.concatenate((far_a, far_b), axis=1)
    both = jnp.concatenate(
        (attended, jnp.concatenate((far[half:], far[:half]), axis=0)), axis=1
    )
    branch_attn = dot_f32(both, jnp.concatenate((out_weight, out_peer), axis=0), NN)
    branch_own = branch_attn[:half]
    middle_own = xf_own + gate_one * branch_own
    middle_peer = xf_peer + gate_one * branch_attn[half:]
    normed_two_f, back_two = jax.vjp(modulate, middle_own, shift_two, scale_two)
    normed_two = jnp.concatenate(
        (normed_two_f.astype(bf16), modulate(middle_peer, shift_two, scale_two).astype(bf16)),
        axis=0,
    )
    grad_out = cotangent[0].astype(jnp.float32)
    grad_mlp = jnp.concatenate(
        (
            (gate_two * grad_out).astype(bf16),
            (gate_two * cot_peer.astype(jnp.float32)).astype(bf16),
        ),
        axis=0,
    )
    hidden_pre = dot_f32(normed_two, up_projection_weight, NN)
    hidden_f, back_gelu = jax.vjp(gelu_tanh, hidden_pre)
    hidden_act = hidden_f.astype(bf16)
    grad_act = dot_f32(grad_mlp, down_projection_weight, NT)
    grad_pre = back_gelu(grad_act)[0].astype(bf16)
    two_recv = swap(dot_f32(grad_pre[half:], up_projection_weight, NT).astype(bf16))
    two_own = dot_f32(grad_pre[:half], up_projection_weight, NT)
    grad_down = dot_f32(hidden_act, grad_mlp, TN).astype(bf16)
    grad_up = dot_f32(normed_two, grad_pre, TN).astype(bf16)
    grad_down, grad_up, two_recv = lax.optimization_barrier((grad_down, grad_up, two_recv))
    sum_down = sum_latents(grad_down, Y_FIRST)
    sum_up = sum_latents(grad_up, Z_FIRST)
    grad_normed_two = two_own + two_recv.astype(jnp.float32)
    middle_back, grad_shift_two, grad_scale_two = back_two(grad_normed_two)
    grad_middle = grad_out + middle_back
    grad_gate_one = jnp.sum(grad_middle * branch_own, axis=0, keepdims=True)
    ga_own = (gate_one * grad_middle).astype(bf16)
    ga_peer = swap(ga_own)
    mlp_far = dot_f32(hidden_act[half:], down_projection_weight, NN).astype(bf16)
    mlp_own = dot_f32(hidden_act[:half], down_projection_weight, NN)
    mlp_far, ga_peer = lax.optimization_barrier((mlp_far, ga_peer))
    branch_mlp = mlp_own + swap(mlp_far).astype(jnp.float32)
    grad_attn = jnp.concatenate((ga_own, ga_peer), axis=0)
    grad_attended = dot_f32(grad_attn, out_weight, NT).astype(bf16)
    grad_out_weight = dot_f32(attended, grad_attn, TN).astype(bf16)
    grad_qkv = attn_backward(qkv, grad_attended, lse)
    one_recv = swap(
        jnp.einsum(
            "ksc,dkc->sd", grad_qkv[:, half:], qkv_weight, preferred_element_type=jnp.float32
        ).astype(bf16)
    )
    one_own = jnp.einsum(
        "ksc,dkc->sd", grad_qkv[:, :half], qkv_weight, preferred_element_type=jnp.float32
    )
    grad_qkv_weight = jnp.einsum(
        "sd,ksc->dkc", normed_one, grad_qkv, preferred_element_type=jnp.float32
    ).astype(bf16)
    sum_out = sum_latents(grad_out_weight, Z_FIRST)
    split = width // 2
    sum_qkv = jnp.concatenate(
        (
            sum_latents(grad_qkv_weight[:split], Y_FIRST),
            sum_latents(grad_qkv_weight[split:], Z_FIRST),
        ),
        axis=0,
    )
    block_out = (middle_own + gate_two * branch_mlp).astype(bf16)
    grad_gate_two = jnp.sum(grad_out * branch_mlp, axis=0, keepdims=True)
    grad_normed_one = one_own + one_recv.astype(jnp.float32)
    inputs_back, grad_shift_one, grad_scale_one = back_one(grad_normed_one)
    grad_inputs = (grad_middle + inputs_back).astype(bf16)
    mod_terms = jnp.concatenate(
        (
            grad_shift_one,
            grad_scale_one,
            grad_gate_one,
            grad_shift_two,
            grad_scale_two,
            grad_gate_two,
        ),
        axis=0,
    )
    left, right = mod_terms[:, :local_cols], mod_terms[:, local_cols:]
    mod_keep = jnp.where(mine == 0, left, right)
    mod_send = jnp.where(mine == 0, right, left).astype(bf16)
    grad_mod = (mod_keep + swap(mod_send).astype(jnp.float32)).astype(bf16)[None]
    factors = lax.all_gather(
        jnp.concatenate((cond_act, grad_mod.reshape(1, 6 * local_cols)), axis=1),
        "dp",
        axis=0,
        tiled=True,
    )
    cond_all = factors[:, :width]
    mod_all = factors[:, width:].reshape(-1, 6, local_cols)
    grad_mod_weight = jnp.einsum(
        "ld,lkc->dkc", cond_all, mod_all, preferred_element_type=jnp.float32
    )
    grad_mod_bias = jnp.sum(mod_all.astype(jnp.float32), axis=0)
    cond_terms = jnp.einsum(
        "lkc,dkc->ld", grad_mod, mod_weight, preferred_element_type=jnp.float32
    )
    grad_conditioning = back_silu(cond_terms + swap(cond_terms))[0]
    return (
        block_out[None],
        grad_inputs[None],
        grad_conditioning,
        grad_mod_weight,
        grad_mod_bias,
        sum_qkv,
        sum_out,
        sum_up,
        sum_down,
    )


def body(inputs, conditioning, mod_weight, mod_bias, qkv_weight, *rest):
    fits = inputs.shape[1] % 256 == 0 and qkv_weight.shape[2] % (4 * HD) == 0
    if lax.axis_size("tensor") == 2 and inputs.shape[0] == 1 and fits:
        return body_pair(inputs, conditioning, mod_weight, mod_bias, qkv_weight, *rest)
    return body_general(inputs, conditioning, mod_weight, mod_bias, qkv_weight, *rest)


def solution(mesh):
    return jax.shard_map(
        body,
        mesh=mesh,
        in_specs=(
            P("dp", "tensor", None),
            P("dp", None),
            P(None, None, "tensor"),
            P(None, "tensor"),
            P(None, None, "tensor"),
            P("tensor", None),
            P(None, "tensor"),
            P("tensor", None),
            P("dp", "tensor", None),
        ),
        out_specs=(
            P("dp", "tensor", None),
            P("dp", "tensor", None),
            P("dp", None),
            P(None, None, "tensor"),
            P(None, "tensor"),
            P(None, None, "tensor"),
            P("tensor", None),
            P(None, "tensor"),
            P("tensor", None),
        ),
        check_vma=False,
    )
```

```python
import jax
import jax.numpy as jnp
from jax import lax
from jax.experimental import pallas as pl
from jax.experimental.pallas import tpu as pltpu
from jax.sharding import PartitionSpec as P

HD = 64


norm_eps = 1e-06


def modulate(values_in, offset, stretch):
    center = jnp.mean(values_in, axis=-1, keepdims=True)
    deviate = values_in - center
    spread = jnp.mean(deviate * deviate, axis=-1, keepdims=True)
    return deviate * lax.rsqrt(spread + norm_eps) * (1.0 + stretch) + offset


def gelu_tanh(values_in):
    return jax.nn.gelu(values_in, approximate=True)


def attend_forward(query, keys, values, scale_factor, block_rows):
    length = query.shape[0]
    blocks = query.reshape(length // block_rows, block_rows, query.shape[1], query.shape[2])

    def one_block(qblock):
        scores = (
            jnp.einsum("qhd,khd->hqk", qblock, keys, preferred_element_type=jnp.float32)
            * scale_factor
        )
        row_peak = jnp.max(scores, axis=-1, keepdims=True)
        exponent = jnp.exp(scores - row_peak)
        row_total = jnp.sum(exponent, axis=-1, keepdims=True)
        shares = (exponent / row_total).astype(jnp.bfloat16)
        result = jnp.einsum("hqk,khd->qhd", shares, values, preferred_element_type=jnp.float32)
        return (result, row_peak[..., 0] + jnp.log(row_total[..., 0]))

    results, log_totals = lax.map(one_block, blocks)
    return (results.reshape(query.shape), log_totals)


def attend_backward(query, keys, values, grad_out, log_totals, scale_factor, block_rows):
    length, head_count, head_size = query.shape
    block_count = length // block_rows
    qblocks = query.reshape(block_count, block_rows, head_count, head_size)
    gblocks = grad_out.reshape(block_count, block_rows, head_count, head_size)

    def one_block(running, pieces):
        grad_keys, grad_values = running
        qblock, gblock, lblock = pieces
        scores = (
            jnp.einsum("qhd,khd->hqk", qblock, keys, preferred_element_type=jnp.float32)
            * scale_factor
        )
        shares = jnp.exp(scores - lblock[..., None])
        grad_shares = jnp.einsum("qhd,khd->hqk", gblock, values, preferred_element_type=jnp.float32)
        inner_sum = jnp.sum(shares * grad_shares, axis=-1, keepdims=True)
        grad_scores = (shares * (grad_shares - inner_sum)).astype(jnp.bfloat16)
        grad_query = (
            jnp.einsum("hqk,khd->qhd", grad_scores, keys, preferred_element_type=jnp.float32)
            * scale_factor
        )
        grad_keys = (
            grad_keys
            + jnp.einsum("hqk,qhd->khd", grad_scores, qblock, preferred_element_type=jnp.float32)
            * scale_factor
        )
        grad_values = grad_values + jnp.einsum(
            "hqk,qhd->khd", shares.astype(jnp.bfloat16), gblock, preferred_element_type=jnp.float32
        )
        return ((grad_keys, grad_values), grad_query.astype(jnp.bfloat16))

    zeroes = jnp.zeros((length, head_count, head_size), jnp.float32)
    finals, grad_query = lax.scan(one_block, (zeroes, zeroes), (qblocks, gblocks, log_totals))
    return (
        grad_query.reshape(query.shape),
        finals[0].astype(jnp.bfloat16),
        finals[1].astype(jnp.bfloat16),
    )


def body_general(
    inputs,
    conditioning,
    mod_weight,
    mod_bias,
    qkv_weight,
    out_weight,
    up_projection_weight,
    down_projection_weight,
    cotangent,
):
    latent_rows, local_len, width = inputs.shape
    local_cols = qkv_weight.shape[2]
    head_count = local_cols // HD
    length = local_len * lax.axis_size("tensor")
    block_rows = min(512, length)
    scale_factor = HD ** (-0.5)
    cond_float = conditioning.astype(jnp.float32)
    cond_silu, back_silu = jax.vjp(jax.nn.silu, cond_float)
    cond_act = cond_silu.astype(jnp.bfloat16)
    mod_local = (
        jnp.einsum("ld,dkc->lkc", cond_act, mod_weight, preferred_element_type=jnp.float32)
        + mod_bias[None]
    )
    modulation = lax.all_gather(mod_local, "tensor", axis=2, tiled=True)
    shift_one = modulation[:, 0:1, :]
    scale_one = modulation[:, 1:2, :]
    gate_one = modulation[:, 2:3, :]
    shift_two = modulation[:, 3:4, :]
    scale_two = modulation[:, 4:5, :]
    gate_two = modulation[:, 5:6, :]
    inputs_float = inputs.astype(jnp.float32)
    normed_float, back_one = jax.vjp(modulate, inputs_float, shift_one, scale_one)
    normed_one = normed_float.astype(jnp.bfloat16)
    normed_all = lax.all_gather(normed_one, "tensor", axis=1, tiled=True)
    projected = jnp.einsum(
        "lsd,dkc->lskc", normed_all, qkv_weight, preferred_element_type=jnp.float32
    ).astype(jnp.bfloat16)
    shaped = projected.reshape(latent_rows, length, 3, head_count, HD)

    def forward_latent(pieces):
        return attend_forward(pieces[:, 0], pieces[:, 1], pieces[:, 2], scale_factor, block_rows)

    attended, log_totals = lax.map(forward_latent, shaped)
    attended = attended.reshape(latent_rows, length, local_cols).astype(jnp.bfloat16)
    attn_terms = jnp.einsum("lsc,cd->lsd", attended, out_weight, preferred_element_type=jnp.float32)
    branch_attn = lax.psum_scatter(
        attn_terms.astype(jnp.bfloat16), "tensor", scatter_dimension=1, tiled=True
    ).astype(jnp.float32)
    middle = inputs_float + gate_one * branch_attn
    normed_float_two, back_two = jax.vjp(modulate, middle, shift_two, scale_two)
    normed_two = normed_float_two.astype(jnp.bfloat16)
    grad_out = cotangent.astype(jnp.float32)
    normed_second_gathered, cot_all = (
        lax.all_gather(normed_two, "tensor", axis=1, tiled=True),
        lax.all_gather(cotangent, "tensor", axis=1, tiled=True),
    )
    hidden_pre = jnp.einsum(
        "vwb,bj->vwj",
        normed_second_gathered,
        up_projection_weight,
        preferred_element_type=jnp.float32,
    )
    hidden_float, back_gelu = jax.vjp(gelu_tanh, hidden_pre)
    hidden_activation = hidden_float.astype(jnp.bfloat16)
    mlp_terms = jnp.einsum(
        "ewy,yz->ewz", hidden_activation, down_projection_weight, preferred_element_type=jnp.float32
    )
    branch_mlp = lax.psum_scatter(
        mlp_terms.astype(jnp.bfloat16), "tensor", scatter_dimension=1, tiled=True
    ).astype(jnp.float32)
    grad_feedforward = (gate_two * cot_all.astype(jnp.float32)).astype(jnp.bfloat16)
    grad_down_projection = jnp.einsum(
        "noi,nok->ik", hidden_activation, grad_feedforward, preferred_element_type=jnp.float32
    )
    grad_activation = jnp.einsum(
        "euz,hz->euh", grad_feedforward, down_projection_weight, preferred_element_type=jnp.float32
    )
    grad_preactivation = back_gelu(grad_activation)[0].astype(jnp.bfloat16)
    grad_up = jnp.einsum(
        "pae,paz->ez",
        normed_second_gathered,
        grad_preactivation,
        preferred_element_type=jnp.float32,
    )
    normed_terms = jnp.einsum(
        "qmt,zt->qmz", grad_preactivation, up_projection_weight, preferred_element_type=jnp.float32
    )
    grad_normed_two = lax.psum_scatter(
        normed_terms.astype(jnp.bfloat16), "tensor", scatter_dimension=1, tiled=True
    ).astype(jnp.float32)
    block_out = (middle + gate_two * branch_mlp).astype(jnp.bfloat16)
    grad_gate_two = jnp.sum(grad_out * branch_mlp, axis=1, keepdims=True)
    middle_back, grad_shift_two, grad_scale_two = back_two(grad_normed_two)
    grad_middle = grad_out + middle_back
    grad_gate_one = jnp.sum(grad_middle * branch_attn, axis=1, keepdims=True)
    grad_attn = (gate_one * grad_middle).astype(jnp.bfloat16)
    grad_attn_all = lax.all_gather(grad_attn, "tensor", axis=1, tiled=True)
    grad_out_weight = jnp.einsum(
        "lsc,lsd->cd", attended, grad_attn_all, preferred_element_type=jnp.float32
    )
    grad_attended = jnp.einsum(
        "lsd,cd->lsc", grad_attn_all, out_weight, preferred_element_type=jnp.float32
    ).astype(jnp.bfloat16)
    grad_shaped = grad_attended.reshape(latent_rows, length, head_count, HD)

    def backward_latent(pieces):
        qkv_rows, grad_rows, totals_rows = pieces
        return attend_backward(
            qkv_rows[:, 0],
            qkv_rows[:, 1],
            qkv_rows[:, 2],
            grad_rows,
            totals_rows,
            scale_factor,
            block_rows,
        )

    grad_query, grad_keys, grad_values = lax.map(backward_latent, (shaped, grad_shaped, log_totals))
    grad_qkv = jnp.stack((grad_query, grad_keys, grad_values), axis=2).reshape(
        latent_rows, length, 3, local_cols
    )
    grad_qkv_weight = jnp.einsum(
        "lsd,lskc->dkc", normed_all, grad_qkv, preferred_element_type=jnp.float32
    )
    normed_one_terms = jnp.einsum(
        "lskc,dkc->lsd", grad_qkv, qkv_weight, preferred_element_type=jnp.float32
    )
    grad_normed_one = lax.psum_scatter(
        normed_one_terms.astype(jnp.bfloat16), "tensor", scatter_dimension=1, tiled=True
    ).astype(jnp.float32)
    inputs_back, grad_shift_one, grad_scale_one = back_one(grad_normed_one)
    grad_inputs = (grad_middle + inputs_back).astype(jnp.bfloat16)
    modulation_terms = jnp.concatenate(
        (
            grad_shift_one,
            grad_scale_one,
            grad_gate_one,
            grad_shift_two,
            grad_scale_two,
            grad_gate_two,
        ),
        axis=1,
    )
    grad_modulation = lax.psum_scatter(
        modulation_terms.astype(jnp.bfloat16), "tensor", scatter_dimension=2, tiled=True
    )
    grad_mod_weight = jnp.einsum(
        "ld,lkc->dkc", cond_act, grad_modulation, preferred_element_type=jnp.float32
    )
    grad_mod_bias = jnp.sum(grad_modulation.astype(jnp.float32), axis=0)
    cond_terms = jnp.einsum(
        "lkc,dkc->ld", grad_modulation, mod_weight, preferred_element_type=jnp.float32
    )
    grad_cond_act = lax.psum(cond_terms, "tensor")
    grad_conditioning = back_silu(grad_cond_act)[0]
    summed = (
        lax.psum(grad_mod_weight.astype(jnp.bfloat16), "dp").astype(jnp.float32),
        lax.psum(grad_mod_bias.astype(jnp.bfloat16), "dp").astype(jnp.float32),
        lax.psum(grad_qkv_weight.astype(jnp.bfloat16), "dp").astype(jnp.float32),
        lax.psum(grad_out_weight.astype(jnp.bfloat16), "dp").astype(jnp.float32),
        lax.psum(grad_up.astype(jnp.bfloat16), "dp").astype(jnp.float32),
        lax.psum(grad_down_projection.astype(jnp.bfloat16), "dp").astype(jnp.float32),
    )
    return (
        block_out,
        grad_inputs,
        grad_conditioning,
        summed[0],
        summed[1],
        summed[2],
        summed[3],
        summed[4],
        summed[5],
    )

LOG2E = 1.4426950408889634
ATT_ROWS = 512


def attn_fwd_kernel(qkv_ref, out_ref, lse_ref):
    length = qkv_ref.shape[1]
    fold = LOG2E * HD ** (-0.5)
    for head in range(2):
        cols = pl.ds(head * HD, HD)
        keys = qkv_ref[1, :, cols]
        values = qkv_ref[2, :, cols]
        for start in range(0, length, ATT_ROWS):
            rows = pl.ds(start, ATT_ROWS)
            query = qkv_ref[0, rows, cols]
            scores = lax.dot_general(
                query, keys, (((1,), (1,)), ((), ())), preferred_element_type=jnp.float32
            )
            peak = jnp.max(scores, axis=-1, keepdims=True)
            exponent = jnp.exp2((scores - peak) * fold)
            total = jnp.sum(exponent, axis=-1, keepdims=True)
            shares = (exponent * (1.0 / total)).astype(jnp.bfloat16)
            result = jnp.dot(shares, values, preferred_element_type=jnp.float32)
            out_ref[rows, cols] = result.astype(jnp.bfloat16)
            log_total = peak * fold + jnp.log2(total)
            flat = jnp.transpose(jnp.broadcast_to(log_total, (ATT_ROWS, 128)))
            lse_ref[0, head : head + 1, rows] = flat[0:1]


def attn_bwd_kernel(qkv_ref, grad_ref, lse_ref, out_ref):
    length = qkv_ref.shape[1]
    scale = HD ** (-0.5)
    fold = LOG2E * scale
    for head in range(2):
        cols = pl.ds(head * HD, HD)
        query = qkv_ref[0, :, cols]
        grad = grad_ref[:, cols]
        lse = lse_ref[0, head : head + 1, :]
        keys = qkv_ref[1, :, cols]
        values = qkv_ref[2, :, cols]
        dk = jnp.zeros((length, HD), jnp.float32)
        dv = jnp.zeros((length, HD), jnp.float32)
        for start in range(0, length, ATT_ROWS):
            qblock = query[start : start + ATT_ROWS]
            gblock = grad[start : start + ATT_ROWS]
            scores = lax.dot_general(
                keys, qblock, (((1,), (1,)), ((), ())), preferred_element_type=jnp.float32
            )
            probs = jnp.exp2(scores * fold - lse[:, start : start + ATT_ROWS])
            dprobs = lax.dot_general(
                values, gblock, (((1,), (1,)), ((), ())), preferred_element_type=jnp.float32
            )
            inner = jnp.sum(probs * dprobs, axis=0, keepdims=True)
            dscores = (probs * (dprobs - inner)).astype(jnp.bfloat16)
            dv = dv + jnp.dot(probs.astype(jnp.bfloat16), gblock, preferred_element_type=jnp.float32)
            dk = dk + jnp.dot(dscores, qblock, preferred_element_type=jnp.float32)
            dq = lax.dot_general(
                dscores, keys, (((0,), (0,)), ((), ())), preferred_element_type=jnp.float32
            )
            out_ref[0, pl.ds(start, ATT_ROWS), cols] = (dq * scale).astype(jnp.bfloat16)
        out_ref[1, :, cols] = (dk * scale).astype(jnp.bfloat16)
        out_ref[2, :, cols] = dv.astype(jnp.bfloat16)


def attn_forward(qkv, first, pairs):
    _, length, _ = qkv.shape
    return pl.pallas_call(
        attn_fwd_kernel,
        grid=(pairs,),
        in_specs=[pl.BlockSpec((3, length, 2 * HD), lambda i: (0, 0, first + i))],
        out_specs=[
            pl.BlockSpec((length, 2 * HD), lambda i: (0, i)),
            pl.BlockSpec((1, 8, length), lambda i: (i, 0, 0)),
        ],
        out_shape=[
            jax.ShapeDtypeStruct((length, pairs * 2 * HD), jnp.bfloat16),
            jax.ShapeDtypeStruct((pairs, 8, length), jnp.float32),
        ],
        compiler_params=pltpu.CompilerParams(vmem_limit_bytes=48 * 1024 * 1024),
        cost_estimate=pl.CostEstimate(
            flops=pairs * 2 * 4 * length * length * HD * 4,
            bytes_accessed=pairs * 8 * length * 2 * HD,
            transcendentals=pairs * 2 * length * length,
        ),
        name="attn_fwd",
    )(qkv)


def attn_backward(qkv, grad, lse):
    _, length, local = qkv.shape
    pairs = local // (2 * HD)
    return pl.pallas_call(
        attn_bwd_kernel,
        grid=(pairs,),
        in_specs=[
            pl.BlockSpec((3, length, 2 * HD), lambda i: (0, 0, i)),
            pl.BlockSpec((length, 2 * HD), lambda i: (0, i)),
            pl.BlockSpec((1, 8, length), lambda i: (i, 0, 0)),
        ],
        out_specs=pl.BlockSpec((3, length, 2 * HD), lambda i: (0, 0, i)),
        out_shape=jax.ShapeDtypeStruct((3, length, local), jnp.bfloat16),
        compiler_params=pltpu.CompilerParams(vmem_limit_bytes=48 * 1024 * 1024),
        cost_estimate=pl.CostEstimate(
            flops=pairs * 2 * 10 * length * length * HD * 4,
            bytes_accessed=pairs * 14 * length * 2 * HD,
            transcendentals=pairs * 2 * length * length,
        ),
        name="attn_bwd",
    )(qkv, grad, lse)


def swap(values_in):
    return lax.ppermute(values_in, "tensor", ((0, 1), (1, 0)))


def sum_latents(values_in, order):
    count = lax.axis_size("dp")
    me = lax.axis_index("dp")
    if count != 16 or values_in.shape[0] % 256 != 0:
        return lax.psum(values_in, "dp").astype(jnp.float32)
    part = values_in
    for bit in order:
        partners = [(i, i ^ bit) for i in range(count)]
        half = part.shape[0] // 2
        mine_at = jnp.where((me & bit) != 0, half, 0)
        sent = lax.dynamic_slice_in_dim(part, half - mine_at, half, 0)
        kept = lax.dynamic_slice_in_dim(part, mine_at, half, 0)
        came = lax.ppermute(sent, "dp", partners)
        part = (kept.astype(jnp.float32) + came.astype(jnp.float32)).astype(jnp.bfloat16)
    for bit in reversed(order):
        partners = [(i, i ^ bit) for i in range(count)]
        came = lax.ppermute(part, "dp", partners)
        part = jnp.where(
            (me & bit) != 0,
            jnp.concatenate((came, part), axis=0),
            jnp.concatenate((part, came), axis=0),
        )
    return part.astype(jnp.float32)


def gather_latents(values_in):
    count = lax.axis_size("dp")
    if count & (count - 1) != 0:
        return lax.all_gather(values_in, "dp", axis=0, tiled=True)
    bit = 1
    while bit < count:
        partners = [(i, i ^ bit) for i in range(count)]
        came = lax.ppermute(values_in, "dp", partners)
        values_in = jnp.concatenate((values_in, came), axis=0)
        bit *= 2
    return values_in


Y_FIRST = (1, 2, 4, 8)
Z_FIRST = (1, 4, 8, 2)


def dot_f32(left, right, dims):
    return lax.dot_general(left, right, (dims, ((), ())), preferred_element_type=jnp.float32)


NN = ((1,), (0,))
NT = ((1,), (1,))
TN = ((0,), (0,))


def body_pair(
    inputs,
    conditioning,
    mod_weight,
    mod_bias,
    qkv_weight,
    out_weight,
    up_projection_weight,
    down_projection_weight,
    cotangent,
):
    bf16 = jnp.bfloat16
    mine = lax.axis_index("tensor")
    x_own = inputs[0]
    half, width = x_own.shape
    local_cols = qkv_weight.shape[2]
    pairs = local_cols // (2 * HD)
    x_peer = swap(x_own)
    cond_silu, back_silu = jax.vjp(jax.nn.silu, conditioning.astype(jnp.float32))
    cond_act = cond_silu.astype(bf16)
    mod_own = (
        jnp.einsum("ld,dkc->lkc", cond_act, mod_weight, preferred_element_type=jnp.float32)
        + mod_bias[None]
    )[0]
    mod_peer = swap(mod_own)
    modulation = jnp.where(
        mine == 0,
        jnp.concatenate((mod_own, mod_peer), axis=1),
        jnp.concatenate((mod_peer, mod_own), axis=1),
    )
    shift_one, scale_one, gate_one, shift_two, scale_two, gate_two = (
        modulation[k : k + 1] for k in range(6)
    )
    xf_own = x_own.astype(jnp.float32)
    normed_own_f, back_one = jax.vjp(modulate, xf_own, shift_one, scale_one)
    normed_own = normed_own_f.astype(bf16)
    cot_later, out_later, x_peer = lax.optimization_barrier((cotangent[0], out_weight, x_peer))
    cot_peer = swap(cot_later)
    out_peer = swap(out_later)
    xf_peer = x_peer.astype(jnp.float32)
    normed_peer = modulate(xf_peer, shift_one, scale_one).astype(bf16)
    normed_one = jnp.concatenate((normed_own, normed_peer), axis=0)
    qkv = jnp.einsum(
        "sd,dkc->ksc", normed_one, qkv_weight, preferred_element_type=jnp.float32
    ).astype(bf16)
    att_a, lse_a = attn_forward(qkv, 0, pairs // 2)
    far_a = swap(att_a)
    att_b, lse_b = attn_forward(qkv, pairs // 2, pairs - pairs // 2)
    far_b = swap(att_b)
    lse = jnp.concatenate((lse_a, lse_b), axis=0)
    attended = jnp.concatenate((att_a, att_b), axis=1)
    far = jnp.concatenate((far_a, far_b), axis=1)
    both = jnp.concatenate(
        (attended, jnp.concatenate((far[half:], far[:half]), axis=0)), axis=1
    )
    branch_attn = dot_f32(both, jnp.concatenate((out_weight, out_peer), axis=0), NN)
    branch_own = branch_attn[:half]
    middle_own = xf_own + gate_one * branch_own
    middle_peer = xf_peer + gate_one * branch_attn[half:]
    normed_two_f, back_two = jax.vjp(modulate, middle_own, shift_two, scale_two)
    normed_two = jnp.concatenate(
        (normed_two_f.astype(bf16), modulate(middle_peer, shift_two, scale_two).astype(bf16)),
        axis=0,
    )
    grad_out = cotangent[0].astype(jnp.float32)
    grad_mlp = jnp.concatenate(
        (
            (gate_two * grad_out).astype(bf16),
            (gate_two * cot_peer.astype(jnp.float32)).astype(bf16),
        ),
        axis=0,
    )
    hidden_pre = dot_f32(normed_two, up_projection_weight, NN)
    hidden_f, back_gelu = jax.vjp(gelu_tanh, hidden_pre)
    hidden_act = hidden_f.astype(bf16)
    grad_act = dot_f32(grad_mlp, down_projection_weight, NT)
    grad_pre = back_gelu(grad_act)[0].astype(bf16)
    two_recv = swap(dot_f32(grad_pre[half:], up_projection_weight, NT).astype(bf16))
    two_own = dot_f32(grad_pre[:half], up_projection_weight, NT)
    grad_down = dot_f32(hidden_act, grad_mlp, TN).astype(bf16)
    grad_up = dot_f32(normed_two, grad_pre, TN).astype(bf16)
    grad_down, grad_up, two_recv = lax.optimization_barrier((grad_down, grad_up, two_recv))
    sum_down, sum_up = lax.psum((grad_down, grad_up), "dp")
    grad_normed_two = two_own + two_recv.astype(jnp.float32)
    middle_back, grad_shift_two, grad_scale_two = back_two(grad_normed_two)
    grad_middle = grad_out + middle_back
    grad_gate_one = jnp.sum(grad_middle * branch_own, axis=0, keepdims=True)
    ga_own = (gate_one * grad_middle).astype(bf16)
    ga_peer = swap(ga_own)
    mlp_far = dot_f32(hidden_act[half:], down_projection_weight, NN).astype(bf16)
    mlp_own = dot_f32(hidden_act[:half], down_projection_weight, NN)
    mlp_far, ga_peer = lax.optimization_barrier((mlp_far, ga_peer))
    branch_mlp = mlp_own + swap(mlp_far).astype(jnp.float32)
    grad_attn = jnp.concatenate((ga_own, ga_peer), axis=0)
    grad_attended = dot_f32(grad_attn, out_weight, NT).astype(bf16)
    grad_out_weight = dot_f32(attended, grad_attn, TN).astype(bf16)
    grad_qkv = attn_backward(qkv, grad_attended, lse)
    one_recv = swap(
        jnp.einsum(
            "ksc,dkc->sd", grad_qkv[:, half:], qkv_weight, preferred_element_type=jnp.float32
        ).astype(bf16)
    )
    one_own = jnp.einsum(
        "ksc,dkc->sd", grad_qkv[:, :half], qkv_weight, preferred_element_type=jnp.float32
    )
    grad_qkv_weight = jnp.einsum(
        "sd,ksc->dkc", normed_one, grad_qkv, preferred_element_type=jnp.float32
    ).astype(bf16)
    sum_out = sum_latents(grad_out_weight, Z_FIRST)
    split = width // 2
    sum_qkv = jnp.concatenate(
        (
            sum_latents(grad_qkv_weight[:split], Y_FIRST),
            sum_latents(grad_qkv_weight[split:], Z_FIRST),
        ),
        axis=0,
    )
    block_out = (middle_own + gate_two * branch_mlp).astype(bf16)
    grad_gate_two = jnp.sum(grad_out * branch_mlp, axis=0, keepdims=True)
    grad_normed_one = one_own + one_recv.astype(jnp.float32)
    inputs_back, grad_shift_one, grad_scale_one = back_one(grad_normed_one)
    grad_inputs = (grad_middle + inputs_back).astype(bf16)
    mod_terms = jnp.concatenate(
        (
            grad_shift_one,
            grad_scale_one,
            grad_gate_one,
            grad_shift_two,
            grad_scale_two,
            grad_gate_two,
        ),
        axis=0,
    )
    left, right = mod_terms[:, :local_cols], mod_terms[:, local_cols:]
    mod_keep = jnp.where(mine == 0, left, right)
    mod_send = jnp.where(mine == 0, right, left).astype(bf16)
    grad_mod = (mod_keep + swap(mod_send).astype(jnp.float32)).astype(bf16)[None]
    factors = gather_latents(
        jnp.concatenate((cond_act, grad_mod.reshape(1, 6 * local_cols)), axis=1)
    )
    cond_all = factors[:, :width]
    mod_all = factors[:, width:].reshape(-1, 6, local_cols)
    grad_mod_weight = jnp.einsum(
        "ld,lkc->dkc", cond_all, mod_all, preferred_element_type=jnp.float32
    )
    grad_mod_bias = jnp.sum(mod_all.astype(jnp.float32), axis=0)
    cond_terms = jnp.einsum(
        "lkc,dkc->ld", grad_mod, mod_weight, preferred_element_type=jnp.float32
    )
    grad_conditioning = back_silu(cond_terms + swap(cond_terms))[0]
    return (
        block_out[None],
        grad_inputs[None],
        grad_conditioning,
        grad_mod_weight,
        grad_mod_bias,
        sum_qkv,
        sum_out,
        sum_up.astype(jnp.float32),
        sum_down.astype(jnp.float32),
    )


def body(inputs, conditioning, mod_weight, mod_bias, qkv_weight, *rest):
    fits = inputs.shape[1] % 256 == 0 and qkv_weight.shape[2] % (4 * HD) == 0
    if lax.axis_size("tensor") == 2 and inputs.shape[0] == 1 and fits:
        return body_pair(inputs, conditioning, mod_weight, mod_bias, qkv_weight, *rest)
    return body_general(inputs, conditioning, mod_weight, mod_bias, qkv_weight, *rest)


def solution(mesh):
    return jax.shard_map(
        body,
        mesh=mesh,
        in_specs=(
            P("dp", "tensor", None),
            P("dp", None),
            P(None, None, "tensor"),
            P(None, "tensor"),
            P(None, None, "tensor"),
            P("tensor", None),
            P(None, "tensor"),
            P("tensor", None),
            P("dp", "tensor", None),
        ),
        out_specs=(
            P("dp", "tensor", None),
            P("dp", "tensor", None),
            P("dp", None),
            P(None, None, "tensor"),
            P(None, "tensor"),
            P(None, None, "tensor"),
            P("tensor", None),
            P(None, "tensor"),
            P("tensor", None),
        ),
        check_vma=False,
    )
```
